256 devices in a mesh: real: 8 (over x_hi, y), strike: 32 (over x_lo, z, core).
Axes of the slice: x: 4 (x_hi: 2, x_lo: 2; x = x_hi * 2 + x_lo), y: 4, z: 8, core: 2. Of those that a mesh axis runs over, the one named last changes fastest.
Arguments:
- grades: bfloat16 [8, 32, 64, 32, 128], P('real', None, 'strike'), may hold values from -6 to 6
- cotangent: bfloat16 [8, 32, 64, 32, 128], P('real', None, 'strike'), may hold values from -6 to 6
- weight: bfloat16 [32, 864], P('real'), may hold values from -0.21875 to 0.21875
- bias: bfloat16 [32], P('real'), may hold values from -3 to 3
Outputs:
- activation: bfloat16 [8, 32, 64, 32, 128], P('real', None, 'strike')
- grad_input: bfloat16 [8, 32, 64, 32, 128], P('real', None, 'strike')
- grad_weight: float32 [32, 864], P('real')
- grad_bias: float32 [32], P('real')
The draws below stay inside these ranges and needn't reach their ends.
All inputs are finite; a program needn't handle non-finite values.
Results may differ from the reference program's by a relative error of at most 0.0095.
Values may be sent and summed in bfloat16 or wider, within the bound.
A program may use at most 128 MiB of HBM per device.

```python
import jax
import jax.numpy as jnp
from jax import lax

CIN = 32
COUT = 32
TAPS = 27
NY = 32
NZ = 128
NX = 64
GROUPS = 8


def block_levels(own_key, shape, pieces, least, top_value):
    factor_of, own = 1.0, jax.random.fold_in(own_key, 6)
    for dim, shards_of in pieces:
        steps = jnp.exp(jax.random.uniform(jax.random.fold_in(own, dim), (shards_of,), jnp.float32, least / len(pieces), top_value / len(pieces)))
        factor_of = factor_of * jnp.repeat(steps, shape[dim] // shards_of).reshape([-1 if axis == dim else 1 for axis in range(len(shape))])
    return factor_of


def bell_draw(own_key, extent, width, limit, pieces=(), held_as=jnp.bfloat16):
    loudness = block_levels(own_key, extent, pieces, -0.22, 0.18) if pieces else 1.0
    array = jax.random.normal(own_key, extent, jnp.float32) * width * loudness
    return jnp.minimum(jnp.maximum(array, -limit), limit).astype(held_as)


def setup_inputs(seed: int = 0) -> dict:
    key_list = jax.random.split(jax.random.key(seed), 5)
    return {
        "grades": bell_draw(key_list[0], (GROUPS, CIN, NX, NY, NZ), 1.0, 6.0, ((0, 8), (2, 32))),
        "cotangent": bell_draw(key_list[1], (GROUPS, COUT, NX, NY, NZ), 1.0, 6.0, ((0, 8), (2, 32))),
        "weight": bell_draw(key_list[2], (COUT, TAPS * CIN), (TAPS * CIN) ** -0.5, 0.21875, ((0, 8),)),
        "bias": bell_draw(key_list[3], (COUT,), 0.5, 3.0, ((0, 8),)),
    }


def conv_field(field, kernel):
    return lax.conv_general_dilated(field[None], kernel, (1, 1, 1), 'SAME', dimension_numbers=('NCDHW', 'OIDHW', 'NCDHW'), precision=lax.Precision.HIGHEST)[0]

def reference(grades, cotangent, weight, bias):
    kernel = weight.astype(jnp.float32).reshape(COUT, 3, 3, 3, CIN).transpose(0, 4, 1, 2, 3)
    bias_vec = bias.astype(jnp.float32)

    def one_group(pair):
        field, cot = pair
        field32 = field.astype(jnp.float32)
        pre = conv_field(field32, kernel) + bias_vec[:, None, None, None]
        sig = jax.nn.sigmoid(pre)
        activation = (pre * sig).astype(jnp.bfloat16)
        dpre = (cot.astype(jnp.float32) * sig * (1.0 + pre * (1.0 - sig))).astype(jnp.bfloat16)
        _, pull = jax.vjp(conv_field, field32, kernel)
        grad_field, grad_kernel = pull(dpre.astype(jnp.float32))
        grad_b = lax.optimization_barrier(jnp.sum(dpre.astype(jnp.float32), axis=(1, 2, 3)))
        return (activation, grad_field.astype(jnp.bfloat16), grad_kernel, grad_b)
    activation, grad_input, kernels, biases = lax.map(one_group, (grades, cotangent))
    factor = 1.0 / (GROUPS * NX * NY * NZ) ** 0.5
    grad_kernel = lax.optimization_barrier(jnp.sum(kernels, axis=0)).transpose(0, 2, 3, 4, 1).reshape(COUT, TAPS * CIN)
    grad_weight = grad_kernel * factor
    grad_bias = lax.optimization_barrier(jnp.sum(biases, axis=0)) * factor
    return (activation, grad_input, grad_weight, grad_bias)
```

```python
import functools

import jax
import jax.numpy as jnp
from jax import lax
from jax.experimental import pallas as pl
from jax.experimental.pallas import tpu as pltpu
from jax.sharding import PartitionSpec as P

MESH = pl.DeviceIdType.MESH
F32 = jnp.float32
BF16 = jnp.bfloat16
CH = 32
NY = 32
NZ = 128
WIDE = 4


def transpose_in(plane, work, put):
    def spread(c, carry):
        work[pl.ds(pl.multiple_of(c * NY, NY), NY), :] = plane(c).astype(F32)
        return carry

    lax.fori_loop(0, CH, spread, 0, unroll=8)

    def gather(y, carry):
        put(y, work[pl.ds(y, CH, NY), :])
        return carry

    lax.fori_loop(0, NY, gather, 0, unroll=8)


def stencil(buf, weights, x, y0):
    pieces = []
    for a in range(3):
        for b in range(3):
            pieces.append(jnp.concatenate([buf[x + a, y0 + j + b] for j in range(WIDE)], axis=1))
    cells = jnp.concatenate(pieces, axis=0)
    product = jnp.dot(weights[...], cells, preferred_element_type=F32)
    lane = lax.broadcasted_iota(jnp.int32, (CH, NZ), 1)
    out = []
    for j in range(WIDE):
        part = product[:, j * NZ : (j + 1) * NZ]
        low = pltpu.roll(part[0:CH], 1, 1)
        high = pltpu.roll(part[2 * CH : 3 * CH], NZ - 1, 1)
        out.append(
            part[CH : 2 * CH]
            + jnp.where(lane == 0, 0.0, low)
            + jnp.where(lane == NZ - 1, 0.0, high)
        )
    return out


def wait_for(ref, sem):
    pltpu.make_async_copy(ref, ref, sem).wait()


def kernel(
    real, xl, zs, co, planes, factor,
    grades, cot, wslot,
    act_out, gin_out, sum_out,
    gv, cv, work, field, dgrad, dshift, wf, wb, bias_col, slots, acc, bias_acc,
    send1, recv1, recv2, piece, act_v, gin_v,
    in_sem, w_send, w_recv, fs, fr, ds, dr, s1, r1, s2, r2, own_sem, out_sem,
):
    strike = xl * zs * co
    quarter = xl * co
    members = real * quarter
    per = CH // members
    me_r, me_s = lax.axis_index("real"), lax.axis_index("strike")
    my_x, my_z, my_c = me_s // (zs * co), lax.rem(me_s // co, zs), lax.rem(me_s, co)
    me_m = me_r * quarter + my_x * co + my_c

    def member(m):
        q = lax.rem(m, quarter)
        return m // quarter, (q // co) * (zs * co) + my_z * co + lax.rem(q, co)

    load_g = pltpu.make_async_copy(grades.at[0], gv, in_sem.at[0])
    load_c = pltpu.make_async_copy(cot.at[0], cv, in_sem.at[1])
    load_g.start()
    load_c.start()

    barrier = pltpu.get_barrier_semaphore()

    def greet_plane(k, carry):
        pl.semaphore_signal(
            barrier, inc=1, device_id=member(lax.rem(me_m + k, members)), device_id_type=MESH
        )
        return carry

    def greet_strike(k, carry):
        pl.semaphore_signal(
            barrier, inc=1, device_id=(me_r, lax.rem(me_s + k, strike)), device_id_type=MESH
        )
        return carry

    lax.fori_loop(1, members, greet_plane, 0)
    lax.fori_loop(1, strike, greet_strike, 0)

    zero = jnp.zeros((CH, NZ), BF16)
    for x in range(planes + 2):
        for buf in (field, dgrad):
            buf[x, 0] = zero
            buf[x, NY + 1] = zero

    def clear(buf, x):
        def row(y, carry):
            buf[x, y + 1] = zero
            return carry

        lax.fori_loop(0, NY, row, 0, unroll=8)

    @pl.when(me_s == 0)
    def _():
        clear(field, 0)
        clear(dgrad, 0)

    @pl.when(me_s == strike - 1)
    def _():
        clear(field, planes + 1)
        clear(dgrad, planes + 1)

    slots[me_r] = wslot[...]
    load_g.wait()
    for x in range(planes):

        def put(y, value, x=x):
            field[x + 1, y + 1] = value.astype(BF16)

        transpose_in(lambda c, x=x: gv[c, x], work, put)

    pl.semaphore_wait(barrier, members - 1 + strike - 1)

    def send_weight(k, carry):
        pltpu.make_async_remote_copy(
            src_ref=wslot,
            dst_ref=slots.at[me_r],
            send_sem=w_send,
            recv_sem=w_recv,
            device_id=(lax.rem(me_r + k, real), me_s),
            device_id_type=MESH,
        ).start()
        return carry

    lax.fori_loop(1, real, send_weight, 0)

    def halo(buf, send, recv, up):
        here, there = (planes, 0) if up else (1, planes + 1)
        i = 0 if up else 1
        return pltpu.make_async_remote_copy(
            src_ref=buf.at[here, pl.ds(1, NY)],
            dst_ref=buf.at[there, pl.ds(1, NY)],
            send_sem=send.at[i],
            recv_sem=recv.at[i],
            device_id=(me_r, me_s + 1 if up else me_s - 1),
            device_id_type=MESH,
        )

    def send_halo(buf, send, recv):
        @pl.when(me_s < strike - 1)
        def _():
            halo(buf, send, recv, True).start()

        @pl.when(me_s > 0)
        def _():
            halo(buf, send, recv, False).start()

    def sent_halo(buf, send):
        @pl.when(me_s < strike - 1)
        def _():
            wait_for(buf.at[planes, pl.ds(1, NY)], send.at[0])

        @pl.when(me_s > 0)
        def _():
            wait_for(buf.at[1, pl.ds(1, NY)], send.at[1])

    def got_halo(buf, recv):
        @pl.when(me_s > 0)
        def _():
            wait_for(buf.at[0, pl.ds(1, NY)], recv.at[0])

        @pl.when(me_s < strike - 1)
        def _():
            wait_for(buf.at[planes + 1, pl.ds(1, NY)], recv.at[1])

    send_halo(field, fs, fr)

    wait_for(slots.at[pl.ds(0, real - 1)], w_recv)
    gathered = slots[...].reshape(128, 256)
    row = lax.broadcasted_iota(jnp.int32, (128, 128), 0)
    col = lax.broadcasted_iota(jnp.int32, (128, 128), 1)
    order = (col == lax.rem(row, CH) * 4 + row // CH).astype(BF16)
    whole = jnp.dot(order, gathered, preferred_element_type=F32)
    turned = jnp.concatenate([whole[:, :128].T, whole[:, 128:].T], axis=0)
    for c in range(3):
        ahead, back = [], []
        for ab in range(9):
            t = 3 * ab + c
            ahead.append(whole[(t // 8) * CH : (t // 8 + 1) * CH, (t % 8) * CH : (t % 8 + 1) * CH])
            t = 26 - t
            back.append(turned[(t % 8) * CH : (t % 8 + 1) * CH, (t // 8) * CH : (t // 8 + 1) * CH])
        wf[pl.ds(c * CH, CH), :] = jnp.concatenate(ahead, axis=1).astype(BF16)
        wb[pl.ds(c * CH, CH), :] = jnp.concatenate(back, axis=1).astype(BF16)
    bias_col[...] = jnp.broadcast_to(whole[96:128, 96:97], (CH, NZ))

    load_c.wait()
    bias_acc[...] = jnp.zeros_like(bias_acc)
    got_halo(field, fr)
    lane = lax.broadcasted_iota(jnp.int32, (CH, NZ), 1)
    for x in range(planes):

        def spread(c, carry, x=x):
            work[pl.ds(pl.multiple_of(c * NY, NY), NY), :] = cv[c, x].astype(F32)
            return carry

        lax.fori_loop(0, CH, spread, 0, unroll=8)

        def forward(step, carry, x=x):
            y0 = step * WIDE
            for j, value in enumerate(stencil(field, wf, x, y0)):
                pre = value + bias_col[...]
                sig = jax.nn.sigmoid(pre)
                gin_v[pl.ds(y0 + j, CH, NY), :] = pre * sig
                upstream = work[pl.ds(y0 + j, CH, NY), :]
                dpre = (upstream * sig * (1.0 + pre * (1.0 - sig))).astype(BF16)
                dgrad[x + 1, y0 + j + 1] = dpre
                wide = dpre.astype(F32)
                bias_acc[...] += wide
                before = jnp.where(lane == NZ - 1, 0.0, pltpu.roll(wide, NZ - 1, 1))
                after = jnp.where(lane == 0, 0.0, pltpu.roll(wide, 1, 1))
                dshift[x, y0 + j] = jnp.concatenate(
                    [before.astype(BF16), dpre, after.astype(BF16)], axis=0
                )
            return carry

        lax.fori_loop(0, NY // WIDE, forward, 0)

        def pack(c, carry, x=x):
            act_v[c, x] = gin_v[pl.ds(pl.multiple_of(c * NY, NY), NY), :].astype(BF16)
            return carry

        lax.fori_loop(0, CH, pack, 0, unroll=8)

    send_halo(dgrad, ds, dr)
    store_act = pltpu.make_async_copy(act_v, act_out.at[0], out_sem.at[0])
    store_act.start()

    acc[...] = jnp.zeros_like(acc)
    for x in range(planes):

        def gram(step, carry, x=x):
            y0 = step * WIDE
            left = jnp.concatenate([dshift[x, y0 + j] for j in range(WIDE)], axis=1)
            pieces = []
            for a in range(3):
                for b in range(3):
                    pieces.append(
                        jnp.concatenate([field[x + a, y0 + j + b] for j in range(WIDE)], axis=1)
                    )
            right = jnp.concatenate(pieces, axis=0)
            acc[...] += lax.dot_general(
                left, right, (((1,), (1,)), ((), ())), preferred_element_type=F32
            )
            return carry

        lax.fori_loop(0, NY // WIDE, gram, 0)

    total = acc[...]
    tails = []
    for c in range(3):
        block = total[c * CH : (c + 1) * CH]
        send1[pl.ds(2 * c, CH, 8), :] = block[:, 0:128]
        send1[pl.ds(2 * c + 1, CH, 8), :] = block[:, 128:256]
        tails.append(block[:, 256:288])
    send1[pl.ds(6, CH, 8), :] = jnp.concatenate(tails + [jnp.zeros((CH, 32), F32)], axis=1)
    send1[pl.ds(7, CH, 8), :] = bias_acc[...]

    rows = per * 8

    def chunk(m):
        return send1.at[pl.ds(pl.multiple_of(m * rows, 8), rows)]

    def scatter(k, carry):
        m = lax.rem(me_m + k, members)
        pltpu.make_async_remote_copy(
            src_ref=chunk(m),
            dst_ref=recv1.at[me_m],
            send_sem=s1,
            recv_sem=r1,
            device_id=member(m),
            device_id_type=MESH,
        ).start()
        return carry

    lax.fori_loop(1, members, scatter, 0)
    own = pltpu.make_async_copy(chunk(me_m), recv1.at[me_m], own_sem)
    own.start()

    def turn_out(x, y, value):
        gin_v[pl.ds(y, CH, NY), :] = value

    got_halo(dgrad, dr)

    def backward(x):
        def step_of(step, carry):
            y0 = step * WIDE
            for j, value in enumerate(stencil(dgrad, wb, x, y0)):
                gin_v[pl.ds(y0 + j, CH, NY), :] = value
            return carry

        lax.fori_loop(0, NY // WIDE, step_of, 0)

        def pack(c, carry):
            gv[c, x] = gin_v[pl.ds(pl.multiple_of(c * NY, NY), NY), :].astype(BF16)
            return carry

        lax.fori_loop(0, CH, pack, 0, unroll=8)

    backward(0)

    own.wait()
    wait_for(recv1.at[pl.ds(0, members - 1)], r1)
    plane_sum = recv1[0]
    for m in range(1, members):
        plane_sum = plane_sum + recv1[m]
    piece[...] = plane_sum
    recv2[me_s] = plane_sum

    def spread_sum(k, carry):
        pltpu.make_async_remote_copy(
            src_ref=piece,
            dst_ref=recv2.at[me_s],
            send_sem=s2,
            recv_sem=r2,
            device_id=(me_r, lax.rem(me_s + k, strike)),
            device_id_type=MESH,
        ).start()
        return carry

    lax.fori_loop(1, strike, spread_sum, 0)

    for x in range(1, planes):
        backward(x)
    store_gin = pltpu.make_async_copy(gv, gin_out.at[0], out_sem.at[1])
    store_gin.start()

    wait_for(recv2.at[pl.ds(0, strike - 1)], r2)
    for xi in range(xl):
        for ci in range(co):
            value = recv2[xi * zs * co + ci]
            for z in range(1, zs):
                value = value + recv2[(xi * zs + z) * co + ci]
            sum_out[xi * co + ci] = value * factor

    wait_for(slots.at[pl.ds(0, real - 1)], w_send)
    sent_halo(field, fs)
    sent_halo(dgrad, ds)
    wait_for(recv1.at[pl.ds(0, members - 1)], s1)
    wait_for(recv2.at[pl.ds(0, strike - 1)], s2)
    store_act.wait()
    store_gin.wait()


def local(grades, cotangent, weight, bias, *, real, xl, zs, co):
    planes = grades.shape[2]
    strike = xl * zs * co
    members = real * xl * co
    per = CH // members
    rows = weight.shape[0]
    cells = real * strike * planes * NY * NZ
    factor = 1.0 / cells**0.5
    wslot = jnp.concatenate(
        [weight, bias[:, None], jnp.zeros((rows, 1024 - 865), BF16)], axis=1
    ).reshape(rows * 4, 256)
    hbm = pl.BlockSpec(memory_space=pl.ANY)
    vmem = pl.BlockSpec(memory_space=pltpu.VMEM)
    block = (1, CH, planes, NY, NZ)
    act, gin, total = pl.pallas_call(
        functools.partial(kernel, real, xl, zs, co, planes, factor),
        out_shape=(
            jax.ShapeDtypeStruct(block, BF16),
            jax.ShapeDtypeStruct(block, BF16),
            jax.ShapeDtypeStruct((xl * co, per * 8, 128), F32),
        ),
        in_specs=[hbm, hbm, vmem],
        out_specs=(hbm, hbm, vmem),
        scratch_shapes=[
            pltpu.VMEM((CH, planes, NY, NZ), BF16),
            pltpu.VMEM((CH, planes, NY, NZ), BF16),
            pltpu.VMEM((CH * NY, NZ), F32),
            pltpu.VMEM((planes + 2, NY + 2, CH, NZ), BF16),
            pltpu.VMEM((planes + 2, NY + 2, CH, NZ), BF16),
            pltpu.VMEM((planes, NY, 3 * CH, NZ), BF16),
            pltpu.VMEM((3 * CH, 9 * CH), BF16),
            pltpu.VMEM((3 * CH, 9 * CH), BF16),
            pltpu.VMEM((CH, NZ), F32),
            pltpu.VMEM((real, rows * 4, 256), BF16),
            pltpu.VMEM((3 * CH, 9 * CH), F32),
            pltpu.VMEM((CH, NZ), F32),
            pltpu.VMEM((CH * 8, 128), F32),
            pltpu.VMEM((members, per * 8, 128), F32),
            pltpu.VMEM((strike, per * 8, 128), F32),
            pltpu.VMEM((per * 8, 128), F32),
            pltpu.VMEM((CH, planes, NY, NZ), BF16),
            pltpu.VMEM((CH * NY, NZ), F32),
            pltpu.SemaphoreType.DMA((2,)),
            pltpu.SemaphoreType.DMA,
            pltpu.SemaphoreType.DMA,
            pltpu.SemaphoreType.DMA((2,)),
            pltpu.SemaphoreType.DMA((2,)),
            pltpu.SemaphoreType.DMA((2,)),
            pltpu.SemaphoreType.DMA((2,)),
            pltpu.SemaphoreType.DMA,
            pltpu.SemaphoreType.DMA,
            pltpu.SemaphoreType.DMA,
            pltpu.SemaphoreType.DMA,
            pltpu.SemaphoreType.DMA,
            pltpu.SemaphoreType.DMA((2,)),
        ],
        compiler_params=pltpu.CompilerParams(
            collective_id=0, has_side_effects=True, vmem_limit_bytes=32 * 1024 * 1024
        ),
    )(grades, cotangent, wslot)
    total = total.reshape(rows, 8, 128)
    taps = jnp.concatenate(
        [total[:, :6].reshape(rows, 3, 256), total[:, 6, :96].reshape(rows, 3, 32)], axis=2
    )
    grad_weight = taps.reshape(rows, 3, 9, 32).transpose(0, 2, 1, 3).reshape(rows, 864)
    grad_bias = jnp.sum(total[:, 7], axis=1)
    return act, gin, grad_weight, grad_bias


def solution(mesh):
    real, strike = mesh.shape["real"], mesh.shape["strike"]
    co = 2
    xl = 2 if strike >= 8 else 1
    zs = strike // (xl * co)
    split = P("real", None, "strike", None, None)
    specs = (split, split, P("real", None), P("real"))
    body = functools.partial(local, real=real, xl=xl, zs=zs, co=co)
    return jax.shard_map(body, mesh=mesh, in_specs=specs, out_specs=specs, check_vma=False)
```

```python
import functools

import jax
import jax.numpy as jnp
from jax import lax
from jax.experimental import pallas as pl
from jax.experimental.pallas import tpu as pltpu
from jax.sharding import PartitionSpec as P

MESH = pl.DeviceIdType.MESH
F32 = jnp.float32
BF16 = jnp.bfloat16
CH = 32
NY = 32
NZ = 128
WIDE = 32


def transpose_in(plane, work, put):
    def spread(c, carry):
        work[pl.ds(pl.multiple_of(c * NY, NY), NY), :] = plane(c).astype(F32)
        return carry

    lax.fori_loop(0, CH, spread, 0, unroll=8)

    def gather(y, carry):
        put(y, work[pl.ds(y, CH, NY), :])
        return carry

    lax.fori_loop(0, NY, gather, 0, unroll=8)


def stencil(buf, weights, x, y0):
    pieces = []
    for a in range(3):
        for b in range(3):
            pieces.append(jnp.concatenate([buf[x + a, y0 + j + b] for j in range(WIDE)], axis=1))
    cells = jnp.concatenate(pieces, axis=0)
    product = jnp.dot(weights[...], cells, preferred_element_type=F32)
    lane = lax.broadcasted_iota(jnp.int32, (CH, NZ), 1)
    for j in range(WIDE):
        part = product[:, j * NZ : (j + 1) * NZ]
        low = pltpu.roll(part[0:CH], 1, 1)
        high = pltpu.roll(part[2 * CH : 3 * CH], NZ - 1, 1)
        yield (
            part[CH : 2 * CH]
            + jnp.where(lane == 0, 0.0, low)
            + jnp.where(lane == NZ - 1, 0.0, high)
        )


def wait_for(ref, sem):
    pltpu.make_async_copy(ref, ref, sem).wait()


def kernel(
    real, xl, zs, co, planes, factor,
    grades, cot, weight, bias,
    act_out, gin_out, sum_out,
    gv, cv, wv, work, turned_out, field, dgrad, dshift, wslot, wf, wb, bias_col, slots, bias_acc,
    send1, recv1, recv2, piece,
    in_sem, w_send, w_recv, fs, fr, ds, dr, s1, r1, s2, r2, own_sem,
):
    strike = xl * zs * co
    quarter = xl * co
    members = real * quarter
    per = CH // members
    me_r, me_s = lax.axis_index("real"), lax.axis_index("strike")
    my_x, my_z, my_c = me_s // (zs * co), lax.rem(me_s // co, zs), lax.rem(me_s, co)
    me_m = me_r * quarter + my_x * co + my_c

    def member(m):
        q = lax.rem(m, quarter)
        return m // quarter, (q // co) * (zs * co) + my_z * co + lax.rem(q, co)

    load_g = pltpu.make_async_copy(grades.at[0], gv, in_sem.at[0])
    load_c = pltpu.make_async_copy(cot.at[0], cv, in_sem.at[1])
    load_w = pltpu.make_async_copy(weight, wv, in_sem.at[2])
    load_w.start()
    load_g.start()
    load_c.start()

    barrier = pltpu.get_barrier_semaphore()

    def greet_plane(k, carry):
        pl.semaphore_signal(
            barrier, inc=1, device_id=member(lax.rem(me_m + k, members)), device_id_type=MESH
        )
        return carry

    def greet_strike(k, carry):
        pl.semaphore_signal(
            barrier, inc=1, device_id=(me_r, lax.rem(me_s + k, strike)), device_id_type=MESH
        )
        return carry

    lax.fori_loop(1, members, greet_plane, 0)
    lax.fori_loop(1, strike, greet_strike, 0)

    zero = jnp.zeros((CH, NZ), BF16)
    for x in range(planes + 2):
        for buf in (field, dgrad):
            buf[x, 0] = zero
            buf[x, NY + 1] = zero

    def clear(buf, x):
        def row(y, carry):
            buf[x, y + 1] = zero
            return carry

        lax.fori_loop(0, NY, row, 0, unroll=8)

    @pl.when(me_s == 0)
    def _():
        clear(field, 0)
        clear(dgrad, 0)

    @pl.when(me_s == strike - 1)
    def _():
        clear(field, planes + 1)
        clear(dgrad, planes + 1)

    rows = CH // real
    load_w.wait()
    taps = wv[...].astype(F32)
    last = jnp.concatenate(
        [taps[:, 768:864], bias[...].astype(F32)[:, :32], jnp.zeros((rows, 128), F32)], axis=1
    )
    wslot[...] = jnp.concatenate(
        [taps[:, 0:256], taps[:, 256:512], taps[:, 512:768], last], axis=0
    ).astype(BF16)
    slots[me_r] = wslot[...]
    load_g.wait()
    for x in range(planes):

        def put(y, value, x=x):
            field[x + 1, y + 1] = value.astype(BF16)

        transpose_in(lambda c, x=x: gv[c, x], work, put)

    pl.semaphore_wait(barrier, members - 1 + strike - 1)

    def send_weight(k, carry):
        pltpu.make_async_remote_copy(
            src_ref=wslot,
            dst_ref=slots.at[me_r],
            send_sem=w_send,
            recv_sem=w_recv,
            device_id=(lax.rem(me_r + k, real), me_s),
            device_id_type=MESH,
        ).start()
        return carry

    lax.fori_loop(1, real, send_weight, 0)

    def halo(buf, send, recv, up):
        here, there = (planes, 0) if up else (1, planes + 1)
        i = 0 if up else 1
        return pltpu.make_async_remote_copy(
            src_ref=buf.at[here, pl.ds(1, NY)],
            dst_ref=buf.at[there, pl.ds(1, NY)],
            send_sem=send.at[i],
            recv_sem=recv.at[i],
            device_id=(me_r, me_s + 1 if up else me_s - 1),
            device_id_type=MESH,
        )

    def send_halo(buf, send, recv):
        @pl.when(me_s < strike - 1)
        def _():
            halo(buf, send, recv, True).start()

        @pl.when(me_s > 0)
        def _():
            halo(buf, send, recv, False).start()

    def sent_halo(buf, send):
        @pl.when(me_s < strike - 1)
        def _():
            wait_for(buf.at[planes, pl.ds(1, NY)], send.at[0])

        @pl.when(me_s > 0)
        def _():
            wait_for(buf.at[1, pl.ds(1, NY)], send.at[1])

    def got_halo(buf, recv):
        @pl.when(me_s > 0)
        def _():
            wait_for(buf.at[0, pl.ds(1, NY)], recv.at[0])

        @pl.when(me_s < strike - 1)
        def _():
            wait_for(buf.at[planes + 1, pl.ds(1, NY)], recv.at[1])

    send_halo(field, fs, fr)

    wait_for(slots.at[pl.ds(0, real - 1)], w_recv)
    gathered = slots[...].reshape(128, 256)
    row = lax.broadcasted_iota(jnp.int32, (128, 128), 0)
    col = lax.broadcasted_iota(jnp.int32, (128, 128), 1)
    out_row, group = lax.rem(row, CH), row // CH
    order = (
        col == (out_row // rows) * (4 * rows) + group * rows + lax.rem(out_row, rows)
    ).astype(BF16)
    whole = jnp.dot(order, gathered, preferred_element_type=F32)
    turned = jnp.concatenate([whole[:, :128].T, whole[:, 128:].T], axis=0)
    for c in range(3):
        ahead, back = [], []
        for ab in range(9):
            t = 3 * ab + c
            ahead.append(whole[(t // 8) * CH : (t // 8 + 1) * CH, (t % 8) * CH : (t % 8 + 1) * CH])
            t = 26 - t
            back.append(turned[(t % 8) * CH : (t % 8 + 1) * CH, (t // 8) * CH : (t // 8 + 1) * CH])
        wf[pl.ds(c * CH, CH), :] = jnp.concatenate(ahead, axis=1).astype(BF16)
        wb[pl.ds(c * CH, CH), :] = jnp.concatenate(back, axis=1).astype(BF16)
    bias_col[...] = jnp.broadcast_to(whole[96:128, 96:97], (CH, NZ))

    load_c.wait()
    bias_acc[...] = jnp.zeros_like(bias_acc)
    got_halo(field, fr)
    lane = lax.broadcasted_iota(jnp.int32, (CH, NZ), 1)
    for x in range(planes):

        def spread(c, carry, x=x):
            work[pl.ds(pl.multiple_of(c * NY, NY), NY), :] = cv[c, x].astype(F32)
            return carry

        lax.fori_loop(0, CH, spread, 0, unroll=8)

        for y, value in enumerate(stencil(field, wf, x, 0)):
            pre = value + bias_col[...]
            sig = jax.nn.sigmoid(pre)
            rise = pre * sig
            turned_out[pl.ds(y, CH, NY), :] = rise
            upstream = work[pl.ds(y, CH, NY), :]
            dpre = (upstream * (sig + rise * (1.0 - sig))).astype(BF16)
            dgrad[x + 1, y + 1] = dpre
            wide = dpre.astype(F32)
            bias_acc[...] += wide
            before = jnp.where(lane == NZ - 1, 0.0, pltpu.roll(wide, NZ - 1, 1))
            after = jnp.where(lane == 0, 0.0, pltpu.roll(wide, 1, 1))
            dshift[x, y, 0:CH] = before.astype(BF16)
            dshift[x, y, CH : 2 * CH] = dpre
            dshift[x, y, 2 * CH : 3 * CH] = after.astype(BF16)

        def pack(c, carry, x=x):
            act_out[0, c, x] = turned_out[pl.ds(pl.multiple_of(c * NY, NY), NY), :].astype(BF16)
            return carry

        lax.fori_loop(0, CH, pack, 0, unroll=8)

    send_halo(dgrad, ds, dr)
    total = None
    for x in range(planes):
        left = jnp.concatenate(
            [
                jnp.concatenate([field[x + a, y + b] for y in range(NY)], axis=1)
                for a in range(3)
                for b in range(3)
            ],
            axis=0,
        )
        right = jnp.concatenate([dshift[x, y] for y in range(NY)], axis=1)
        part = lax.dot_general(left, right, (((1,), (1,)), ((), ())), preferred_element_type=F32)
        total = part if total is None else total + part
    total = jnp.concatenate([total, jnp.zeros((9 * CH, CH), F32)], axis=1)
    total = jnp.concatenate([total, jnp.zeros((3 * CH, 4 * CH), F32)], axis=0)
    total = jnp.concatenate(
        [total[k * 128 : (k + 1) * 128].T for k in range(3)], axis=1
    )
    tails = []
    for c in range(3):
        block = total[c * CH : (c + 1) * CH]
        send1[pl.ds(2 * c, CH, 8), :] = block[:, 0:128]
        send1[pl.ds(2 * c + 1, CH, 8), :] = block[:, 128:256]
        tails.append(block[:, 256:288])
    send1[pl.ds(6, CH, 8), :] = jnp.concatenate(tails + [jnp.zeros((CH, 32), F32)], axis=1)
    send1[pl.ds(7, CH, 8), :] = bias_acc[...]

    tile = per * 8

    def chunk(m):
        return send1.at[pl.ds(pl.multiple_of(m * tile, 8), tile)]

    def scatter(k, carry):
        m = lax.rem(me_m + k, members)
        pltpu.make_async_remote_copy(
            src_ref=chunk(m),
            dst_ref=recv1.at[me_m],
            send_sem=s1,
            recv_sem=r1,
            device_id=member(m),
            device_id_type=MESH,
        ).start()
        return carry

    lax.fori_loop(1, members, scatter, 0)
    own = pltpu.make_async_copy(chunk(me_m), recv1.at[me_m], own_sem)
    own.start()

    got_halo(dgrad, dr)

    def backward(x):
        for y, value in enumerate(stencil(dgrad, wb, x, 0)):
            turned_out[pl.ds(y, CH, NY), :] = value

        def pack(c, carry):
            gin_out[0, c, x] = turned_out[pl.ds(pl.multiple_of(c * NY, NY), NY), :].astype(BF16)
            return carry

        lax.fori_loop(0, CH, pack, 0, unroll=8)

    backward(0)

    own.wait()
    wait_for(recv1.at[pl.ds(0, members - 1)], r1)
    plane_sum = recv1[0]
    for m in range(1, members):
        plane_sum = plane_sum + recv1[m]
    piece[...] = plane_sum
    recv2[me_s] = plane_sum

    def spread_sum(k, carry):
        pltpu.make_async_remote_copy(
            src_ref=piece,
            dst_ref=recv2.at[me_s],
            send_sem=s2,
            recv_sem=r2,
            device_id=(me_r, lax.rem(me_s + k, strike)),
            device_id_type=MESH,
        ).start()
        return carry

    lax.fori_loop(1, strike, spread_sum, 0)

    for x in range(1, planes):
        backward(x)

    wait_for(recv2.at[pl.ds(0, strike - 1)], r2)
    for xi in range(xl):
        for ci in range(co):
            value = recv2[xi * zs * co + ci]
            for z in range(1, zs):
                value = value + recv2[(xi * zs + z) * co + ci]
            sum_out[pl.ds((xi * co + ci) * tile, tile), :] = value * factor

    wait_for(slots.at[pl.ds(0, real - 1)], w_send)
    sent_halo(field, fs)
    sent_halo(dgrad, ds)
    wait_for(recv1.at[pl.ds(0, members - 1)], s1)
    wait_for(recv2.at[pl.ds(0, strike - 1)], s2)


def place(rows, act, gin, total, act_out, gin_out, weight_out, bias_out, sems):
    move_act = pltpu.make_async_copy(act, act_out, sems.at[0])
    move_gin = pltpu.make_async_copy(gin, gin_out, sems.at[1])
    move_act.start()
    move_gin.start()
    parts = [total[pl.ds(g, rows, 8), :] for g in range(8)]
    taps = []
    for ab in range(9):
        for c in range(3):
            if ab < 8:
                source, at = parts[2 * c + ab // 4], (ab % 4) * 32
            else:
                source, at = parts[6], c * 32
            taps.append(source[:, at : at + 32])
    weight_out[...] = jnp.concatenate(taps, axis=1)
    bias_out[...] = jnp.sum(parts[7], axis=1, keepdims=True)
    move_act.wait()
    move_gin.wait()


def local(grades, cotangent, weight, bias, *, real, xl, zs, co):
    planes = grades.shape[2]
    strike = xl * zs * co
    members = real * xl * co
    per = CH // members
    rows = weight.shape[0]
    cells = real * strike * planes * NY * NZ
    factor = 1.0 / cells**0.5
    hbm = pl.BlockSpec(memory_space=pltpu.HBM)
    vmem = pl.BlockSpec(memory_space=pltpu.VMEM)
    block = jax.ShapeDtypeStruct((1, CH, planes, NY, NZ), BF16)
    scratch = [
        ((CH, planes, NY, NZ), BF16),
        ((CH, planes, NY, NZ), BF16),
        ((rows, 27 * CH), BF16),
        ((CH * NY, NZ), F32),
        ((CH * NY, NZ), F32),
        ((planes + 2, NY + 2, CH, NZ), BF16),
        ((planes + 2, NY + 2, CH, NZ), BF16),
        ((planes, NY, 3 * CH, NZ), BF16),
        ((rows * 4, 256), BF16),
        ((3 * CH, 9 * CH), BF16),
        ((3 * CH, 9 * CH), BF16),
        ((CH, NZ), F32),
        ((real, rows * 4, 256), BF16),
        ((CH, NZ), F32),
        ((CH * 8, 128), F32),
        ((members, per * 8, 128), F32),
        ((strike, per * 8, 128), F32),
        ((per * 8, 128), F32),
    ]
    pair, single = pltpu.SemaphoreType.DMA((2,)), pltpu.SemaphoreType.DMA
    act, gin, total = pl.pallas_call(
        functools.partial(kernel, real, xl, zs, co, planes, factor),
        out_shape=(block, block, jax.ShapeDtypeStruct((rows * 8, 128), F32)),
        in_specs=[hbm, hbm, hbm, vmem],
        out_specs=(vmem, vmem, vmem),
        scratch_shapes=[pltpu.VMEM(*each) for each in scratch]
        + [pltpu.SemaphoreType.DMA((3,)), single, single, pair, pair, pair, pair] + [single] * 5,
        compiler_params=pltpu.CompilerParams(
            collective_id=0, has_side_effects=True, vmem_limit_bytes=32 * 1024 * 1024
        ),
    )(
        pltpu.with_memory_space_constraint(grades, pltpu.HBM),
        pltpu.with_memory_space_constraint(cotangent, pltpu.HBM),
        pltpu.with_memory_space_constraint(weight, pltpu.HBM),
        jnp.broadcast_to(bias[:, None], (rows, 128)),
    )
    act, gin, grad_weight, grad_bias = pl.pallas_call(
        functools.partial(place, rows),
        out_shape=(
            block,
            block,
            jax.ShapeDtypeStruct((rows, 27 * CH), F32),
            jax.ShapeDtypeStruct((rows, 1), F32),
        ),
        in_specs=[vmem, vmem, vmem],
        out_specs=(hbm, hbm, vmem, vmem),
        scratch_shapes=[pair],
        compiler_params=pltpu.CompilerParams(vmem_limit_bytes=4 * 1024 * 1024),
    )(act, gin, total)
    return act, gin, grad_weight, grad_bias.reshape(rows)


def solution(mesh):
    real, strike = mesh.shape["real"], mesh.shape["strike"]
    co = 2
    xl = 2 if strike >= 8 else 1
    zs = strike // (xl * co)
    split = P("real", None, "strike", None, None)
    specs = (split, split, P("real", None), P("real"))
    body = functools.partial(local, real=real, xl=xl, zs=zs, co=co)
    return jax.shard_map(body, mesh=mesh, in_specs=specs, out_specs=specs, check_vma=False)
```

```python
import functools

import jax
import jax.numpy as jnp
from jax import lax
from jax.experimental import pallas as pl
from jax.experimental.pallas import tpu as pltpu
from jax.sharding import PartitionSpec as P

MESH = pl.DeviceIdType.MESH
F32 = jnp.float32
BF16 = jnp.bfloat16
CH = 32
NY = 32
NZ = 128


def transpose_in(plane, work, put):
    def spread(c, carry):
        work[pl.ds(pl.multiple_of(c * NY, NY), NY), :] = plane(c).astype(F32)
        return carry

    lax.fori_loop(0, CH, spread, 0, unroll=8)

    def gather(y, carry):
        put(y, work[pl.ds(y, CH, NY), :])
        return carry

    lax.fori_loop(0, NY, gather, 0, unroll=8)


def stencil(buf, weights, x, near):
    pieces = []
    for a in near:
        for b in range(3):
            pieces.append(jnp.concatenate([buf[x + a, y + b] for y in range(NY)], axis=1))
    cells = jnp.concatenate(pieces, axis=0)
    columns = slice(near[0] * 3 * CH, (near[-1] + 1) * 3 * CH)
    product = jnp.dot(weights[:, columns], cells, preferred_element_type=F32)
    lane = lax.broadcasted_iota(jnp.int32, (CH, NZ), 1)
    for y in range(NY):
        part = product[:, y * NZ : (y + 1) * NZ]
        low = pltpu.roll(part[0:CH], 1, 1)
        high = pltpu.roll(part[2 * CH : 3 * CH], NZ - 1, 1)
        yield (
            part[CH : 2 * CH]
            + jnp.where(lane == 0, 0.0, low)
            + jnp.where(lane == NZ - 1, 0.0, high)
        )


def wait_for(ref, sem):
    pltpu.make_async_copy(ref, ref, sem).wait()


def kernel(
    real, xl, zs, co, planes, factor,
    grades, cot, weight, bias,
    act_out, gin_out, sum_out,
    gv, cv, wv, bv, work, turned_out, partial, field, dgrad, dshift, wslot, wf, wb, bias_col, slots,
    send1, recv1, recv2, piece,
    in_sem, w_send, w_recv, fs, fr, ds, dr, s1, r1, s2, r2, own_sem,
):
    strike = xl * zs * co
    quarter = xl * co
    members = real * quarter
    per = CH // members
    me_r, me_s = lax.axis_index("real"), lax.axis_index("strike")
    my_x, my_z, my_c = me_s // (zs * co), lax.rem(me_s // co, zs), lax.rem(me_s, co)
    me_m = me_r * quarter + my_x * co + my_c

    def member(m):
        q = lax.rem(m, quarter)
        return m // quarter, (q // co) * (zs * co) + my_z * co + lax.rem(q, co)

    load_g = pltpu.make_async_copy(grades.at[0], gv, in_sem.at[0])
    load_c = pltpu.make_async_copy(cot.at[0], cv, in_sem.at[1])
    load_w = pltpu.make_async_copy(weight, wv, in_sem.at[2])
    load_b = pltpu.make_async_copy(bias, bv, in_sem.at[3])
    load_w.start()
    load_b.start()
    load_g.start()
    load_c.start()

    barrier = pltpu.get_barrier_semaphore()

    def greet_plane(k, carry):
        pl.semaphore_signal(
            barrier, inc=1, device_id=member(lax.rem(me_m + k, members)), device_id_type=MESH
        )
        return carry

    def greet_strike(k, carry):
        pl.semaphore_signal(
            barrier, inc=1, device_id=(me_r, lax.rem(me_s + k, strike)), device_id_type=MESH
        )
        return carry

    lax.fori_loop(1, members, greet_plane, 0)
    lax.fori_loop(1, strike, greet_strike, 0)

    zero = jnp.zeros((CH, NZ), BF16)
    for x in range(planes + 2):
        for buf in (field, dgrad):
            buf[x, 0] = zero
            buf[x, NY + 1] = zero

    def clear(buf, x):
        def row(y, carry):
            buf[x, y + 1] = zero
            return carry

        lax.fori_loop(0, NY, row, 0, unroll=8)

    @pl.when(me_s == 0)
    def _():
        clear(field, 0)
        clear(dgrad, 0)

    @pl.when(me_s == strike - 1)
    def _():
        clear(field, planes + 1)
        clear(dgrad, planes + 1)

    rows = CH // real
    load_w.wait()
    load_b.wait()
    taps = wv[...].astype(F32)
    here = lax.broadcasted_iota(jnp.int32, (rows, rows), 0)
    there = lax.broadcasted_iota(jnp.int32, (rows, rows), 1)
    diagonal = jnp.where(here == there, jnp.broadcast_to(bv[...].astype(F32), (rows, rows)), 0.0)
    last = jnp.concatenate(
        [taps[:, 768:864], diagonal, jnp.zeros((rows, 160 - rows), F32)], axis=1
    )
    wslot[...] = jnp.concatenate(
        [taps[:, 0:256], taps[:, 256:512], taps[:, 512:768], last], axis=0
    ).astype(BF16)
    slots[me_r] = wslot[...]
    load_g.wait()
    for x in range(planes):

        def put(y, value, x=x):
            field[x + 1, y + 1] = value.astype(BF16)

        transpose_in(lambda c, x=x: gv[c, x], work, put)

    pl.semaphore_wait(barrier, members - 1 + strike - 1)

    wide_y = real // 2
    my_xh, my_y = me_r // wide_y, lax.rem(me_r, wide_y)

    def send_weight(k, carry):
        across = k // wide_y
        to_r = lax.rem(my_xh + across, 2) * wide_y + lax.rem(my_y + lax.rem(k, wide_y), wide_y)
        to_s = lax.rem(my_x + across, xl) * (zs * co) + my_z * co + my_c
        pltpu.make_async_remote_copy(
            src_ref=wslot,
            dst_ref=slots.at[me_r],
            send_sem=w_send,
            recv_sem=w_recv,
            device_id=(to_r, to_s),
            device_id_type=MESH,
        ).start()
        return carry

    lax.fori_loop(1, real, send_weight, 0)

    def halo(buf, send, recv, up):
        here, there = (planes, 0) if up else (1, planes + 1)
        i = 0 if up else 1
        return pltpu.make_async_remote_copy(
            src_ref=buf.at[here, pl.ds(1, NY)],
            dst_ref=buf.at[there, pl.ds(1, NY)],
            send_sem=send.at[i],
            recv_sem=recv.at[i],
            device_id=(me_r, me_s + 1 if up else me_s - 1),
            device_id_type=MESH,
        )

    def send_halo(buf, send, recv):
        @pl.when(me_s < strike - 1)
        def _():
            halo(buf, send, recv, True).start()

        @pl.when(me_s > 0)
        def _():
            halo(buf, send, recv, False).start()

    def sent_halo(buf, send):
        @pl.when(me_s < strike - 1)
        def _():
            wait_for(buf.at[planes, pl.ds(1, NY)], send.at[0])

        @pl.when(me_s > 0)
        def _():
            wait_for(buf.at[1, pl.ds(1, NY)], send.at[1])

    def got_below(buf, recv):
        @pl.when(me_s > 0)
        def _():
            wait_for(buf.at[0, pl.ds(1, NY)], recv.at[0])

    def got_above(buf, recv):
        @pl.when(me_s < strike - 1)
        def _():
            wait_for(buf.at[planes + 1, pl.ds(1, NY)], recv.at[1])

    send_halo(field, fs, fr)

    wait_for(slots.at[pl.ds(0, real - 1)], w_recv)
    gathered = slots[...].reshape(128, 256)
    row = lax.broadcasted_iota(jnp.int32, (128, 128), 0)
    col = lax.broadcasted_iota(jnp.int32, (128, 128), 1)
    out_row, group = lax.rem(row, CH), row // CH
    order = (
        col == (out_row // rows) * (4 * rows) + group * rows + lax.rem(out_row, rows)
    ).astype(BF16)
    whole = jnp.dot(order, gathered, preferred_element_type=F32)
    for c in range(3):
        ahead = []
        for ab in range(9):
            t = 3 * ab + c
            ahead.append(whole[(t // 8) * CH : (t // 8 + 1) * CH, (t % 8) * CH : (t % 8 + 1) * CH])
        wf[pl.ds(c * CH, CH), :] = jnp.concatenate(ahead, axis=1).astype(BF16)
    bias_col[...] = jnp.broadcast_to(
        jnp.sum(whole[96:128, 96 : 96 + rows], axis=1, keepdims=True), (CH, NZ)
    )

    lane = lax.broadcasted_iota(jnp.int32, (CH, NZ), 1)
    sides = ((1, 2), (0, 1))
    edges = ((0,), (2,))
    for x in range(planes):
        for y, value in enumerate(stencil(field, wf, x, sides[x])):
            partial[x, y] = value + bias_col[...]

    load_c.wait()
    bias_sum = jnp.zeros((CH, NZ), F32)
    for x in range(planes):

        def spread(c, carry, x=x):
            work[pl.ds(pl.multiple_of(c * NY, NY), NY), :] = cv[c, x].astype(F32)
            return carry

        lax.fori_loop(0, CH, spread, 0, unroll=8)
        (got_below if x == 0 else got_above)(field, fr)
        for y, value in enumerate(stencil(field, wf, x, edges[x])):
            pre = value + partial[x, y]
            sig = jax.nn.sigmoid(pre)
            rise = pre * sig
            turned_out[pl.ds(x * CH * NY + y, CH, NY), :] = rise
            upstream = work[pl.ds(y, CH, NY), :]
            dpre = (upstream * (sig + rise * (1.0 - sig))).astype(BF16)
            dgrad[x + 1, y + 1] = dpre
            wide = dpre.astype(F32)
            bias_sum = bias_sum + wide
            before = jnp.where(lane == NZ - 1, 0.0, pltpu.roll(wide, NZ - 1, 1))
            after = jnp.where(lane == 0, 0.0, pltpu.roll(wide, 1, 1))
            dshift[x, y, 0:CH] = before.astype(BF16)
            dshift[x, y, CH : 2 * CH] = dpre
            dshift[x, y, 2 * CH : 3 * CH] = after.astype(BF16)

    send_halo(dgrad, ds, dr)
    total = None
    for x in range(planes):
        left = jnp.concatenate(
            [
                jnp.concatenate([field[x + a, y + b] for y in range(NY)], axis=1)
                for a in range(3)
                for b in range(3)
            ],
            axis=0,
        )
        right = jnp.concatenate([dshift[x, y] for y in range(NY)], axis=1)
        part = lax.dot_general(left, right, (((1,), (1,)), ((), ())), preferred_element_type=F32)
        total = part if total is None else total + part
    total = jnp.concatenate([total, jnp.zeros((9 * CH, CH), F32)], axis=1)
    total = jnp.concatenate([total, jnp.zeros((3 * CH, 4 * CH), F32)], axis=0)
    total = jnp.concatenate(
        [total[k * 128 : (k + 1) * 128].T for k in range(3)], axis=1
    )
    tails = []
    for c in range(3):
        block = total[c * CH : (c + 1) * CH]
        send1[pl.ds(2 * c, CH, 8), :] = block[:, 0:128]
        send1[pl.ds(2 * c + 1, CH, 8), :] = block[:, 128:256]
        tails.append(block[:, 256:288])
    send1[pl.ds(6, CH, 8), :] = jnp.concatenate(tails + [jnp.zeros((CH, 32), F32)], axis=1)
    send1[pl.ds(7, CH, 8), :] = bias_sum

    tile = per * 8

    def chunk(m):
        return send1.at[pl.ds(pl.multiple_of(m * tile, 8), tile)]

    def scatter(k, carry):
        m = lax.rem(me_m + k, members)
        pltpu.make_async_remote_copy(
            src_ref=chunk(m),
            dst_ref=recv1.at[me_m],
            send_sem=s1,
            recv_sem=r1,
            device_id=member(m),
            device_id_type=MESH,
        ).start()
        return carry

    lax.fori_loop(1, members, scatter, 0)
    own = pltpu.make_async_copy(chunk(me_m), recv1.at[me_m], own_sem)
    own.start()

    def pack(out):
        for x in range(planes):

            def channel(c, carry, x=x):
                rows_of = pl.ds(pl.multiple_of(x * CH * NY + c * NY, NY), NY)
                out[0, c, x] = turned_out[rows_of, :].astype(BF16)
                return carry

            lax.fori_loop(0, CH, channel, 0, unroll=8)

    pack(act_out)
    turned = jnp.concatenate([whole[:, :128].T, whole[:, 128:].T], axis=0)
    for c in range(3):
        back = []
        for ab in range(9):
            t = 26 - (3 * ab + c)
            back.append(turned[(t % 8) * CH : (t % 8 + 1) * CH, (t // 8) * CH : (t // 8 + 1) * CH])
        wb[pl.ds(c * CH, CH), :] = jnp.concatenate(back, axis=1).astype(BF16)
    for x in range(planes):
        for y, value in enumerate(stencil(dgrad, wb, x, sides[x])):
            partial[x, y] = value

    own.wait()
    wait_for(recv1.at[pl.ds(0, members - 1)], r1)
    plane_sum = recv1[0]
    for m in range(1, members):
        plane_sum = plane_sum + recv1[m]
    piece[...] = plane_sum.astype(BF16)
    recv2[me_s] = plane_sum.astype(BF16)

    def spread_sum(k, carry):
        pltpu.make_async_remote_copy(
            src_ref=piece,
            dst_ref=recv2.at[me_s],
            send_sem=s2,
            recv_sem=r2,
            device_id=(me_r, lax.rem(me_s + k, strike)),
            device_id_type=MESH,
        ).start()
        return carry

    lax.fori_loop(1, strike, spread_sum, 0)

    for x in range(planes):
        (got_below if x == 0 else got_above)(dgrad, dr)
        for y, value in enumerate(stencil(dgrad, wb, x, edges[x])):
            turned_out[pl.ds(x * CH * NY + y, CH, NY), :] = value + partial[x, y]
    pack(gin_out)

    wait_for(recv2.at[pl.ds(0, strike - 1)], r2)
    for xi in range(xl):
        for ci in range(co):
            value = recv2[xi * zs * co + ci].astype(F32)
            for z in range(1, zs):
                value = value + recv2[(xi * zs + z) * co + ci].astype(F32)
            sum_out[pl.ds((xi * co + ci) * tile, tile), :] = value * factor

    wait_for(slots.at[pl.ds(0, real - 1)], w_send)
    sent_halo(field, fs)
    sent_halo(dgrad, ds)
    wait_for(recv1.at[pl.ds(0, members - 1)], s1)
    wait_for(recv2.at[pl.ds(0, strike - 1)], s2)


def place(rows, act, gin, total, act_out, gin_out, weight_out, bias_out, taps_v, sums_v, sems):
    results = ((act, act_out), (gin, gin_out), (taps_v, weight_out), (sums_v, bias_out))
    moves = [
        pltpu.make_async_copy(held, out, sems.at[i]) for i, (held, out) in enumerate(results)
    ]
    moves[0].start()
    moves[1].start()
    parts = [total[pl.ds(g, rows, 8), :] for g in range(8)]
    taps = []
    for ab in range(9):
        for c in range(3):
            if ab < 8:
                source, at = parts[2 * c + ab // 4], (ab % 4) * 32
            else:
                source, at = parts[6], c * 32
            taps.append(source[:, at : at + 32])
    taps_v[...] = jnp.concatenate(taps, axis=1)
    sums = jnp.broadcast_to(jnp.sum(parts[7], axis=1, keepdims=True), (rows, 128))
    here = lax.broadcasted_iota(jnp.int32, (rows, 128), 0)
    there = lax.broadcasted_iota(jnp.int32, (rows, 128), 1)
    line = jnp.sum(jnp.where(here == there, sums, 0.0), axis=0, keepdims=True)
    sums_v[...] = line[:, :rows]
    moves[2].start()
    moves[3].start()
    for move in moves:
        move.wait()


def local(grades, cotangent, weight, bias, *, real, xl, zs, co):
    planes = grades.shape[2]
    strike = xl * zs * co
    members = real * xl * co
    per = CH // members
    rows = weight.shape[0]
    cells = real * strike * planes * NY * NZ
    factor = 1.0 / cells**0.5
    hbm = pl.BlockSpec(memory_space=pltpu.HBM)
    vmem = pl.BlockSpec(memory_space=pltpu.VMEM)
    block = jax.ShapeDtypeStruct((1, CH, planes, NY, NZ), BF16)
    scratch = [
        ((CH, planes, NY, NZ), BF16),
        ((CH, planes, NY, NZ), BF16),
        ((rows, 27 * CH), BF16),
        ((1, rows), BF16),
        ((CH * NY, NZ), F32),
        ((planes * CH * NY, NZ), F32),
        ((planes, NY, CH, NZ), F32),
        ((planes + 2, NY + 2, CH, NZ), BF16),
        ((planes + 2, NY + 2, CH, NZ), BF16),
        ((planes, NY, 3 * CH, NZ), BF16),
        ((rows * 4, 256), BF16),
        ((3 * CH, 9 * CH), BF16),
        ((3 * CH, 9 * CH), BF16),
        ((CH, NZ), F32),
        ((real, rows * 4, 256), BF16),
        ((CH * 8, 128), F32),
        ((members, per * 8, 128), F32),
        ((strike, per * 8, 128), BF16),
        ((per * 8, 128), BF16),
    ]
    pair, single = pltpu.SemaphoreType.DMA((2,)), pltpu.SemaphoreType.DMA
    act, gin, total = pl.pallas_call(
        functools.partial(kernel, real, xl, zs, co, planes, factor),
        out_shape=(block, block, jax.ShapeDtypeStruct((rows * 8, 128), F32)),
        in_specs=[hbm, hbm, hbm, hbm],
        out_specs=(vmem, vmem, vmem),
        scratch_shapes=[pltpu.VMEM(*each) for each in scratch]
        + [pltpu.SemaphoreType.DMA((4,)), single, single, pair, pair, pair, pair] + [single] * 5,
        compiler_params=pltpu.CompilerParams(
            collective_id=0, has_side_effects=True, vmem_limit_bytes=32 * 1024 * 1024
        ),
    )(
        pltpu.with_memory_space_constraint(grades, pltpu.HBM),
        pltpu.with_memory_space_constraint(cotangent, pltpu.HBM),
        pltpu.with_memory_space_constraint(weight, pltpu.HBM),
        pltpu.with_memory_space_constraint(bias.reshape(1, rows), pltpu.HBM),
    )
    act, gin, grad_weight, grad_bias = pl.pallas_call(
        functools.partial(place, rows),
        out_shape=(
            block,
            block,
            jax.ShapeDtypeStruct((rows, 27 * CH), F32),
            jax.ShapeDtypeStruct((1, rows), F32),
        ),
        in_specs=[vmem, vmem, vmem],
        out_specs=(hbm, hbm, hbm, hbm),
        scratch_shapes=[
            pltpu.VMEM((rows, 27 * CH), F32),
            pltpu.VMEM((1, rows), F32),
            pltpu.SemaphoreType.DMA((4,)),
        ],
        compiler_params=pltpu.CompilerParams(vmem_limit_bytes=4 * 1024 * 1024),
    )(act, gin, total)
    return act, gin, grad_weight, grad_bias.reshape(rows)


def solution(mesh):
    real, strike = mesh.shape["real"], mesh.shape["strike"]
    co = 2
    xl = 2 if strike >= 8 else 1
    zs = strike // (xl * co)
    split = P("real", None, "strike", None, None)
    specs = (split, split, P("real", None), P("real"))
    body = functools.partial(local, real=real, xl=xl, zs=zs, co=co)
    return jax.shard_map(body, mesh=mesh, in_specs=specs, out_specs=specs, check_vma=False)
```

```python
import functools

import jax
import jax.numpy as jnp
from jax import lax
from jax.experimental import pallas as pl
from jax.experimental.pallas import tpu as pltpu
from jax.sharding import PartitionSpec as P

MESH = pl.DeviceIdType.MESH
F32 = jnp.float32
BF16 = jnp.bfloat16
CH = 32
NY = 32
NZ = 128


def transpose_in(plane, work, put):
    def spread(c, carry):
        work[pl.ds(pl.multiple_of(c * NY, NY), NY), :] = plane(c).astype(F32)
        return carry

    lax.fori_loop(0, CH, spread, 0, unroll=8)

    def gather(y, carry):
        put(y, work[pl.ds(y, CH, NY), :])
        return carry

    lax.fori_loop(0, NY, gather, 0, unroll=8)


def stencil(buf, weights, x, near):
    pieces = []
    for a in near:
        for b in range(3):
            pieces.append(jnp.concatenate([buf[x + a, y + b] for y in range(NY)], axis=1))
    cells = jnp.concatenate(pieces, axis=0)
    columns = slice(near[0] * 3 * CH, (near[-1] + 1) * 3 * CH)
    product = jnp.dot(weights[:, columns], cells, preferred_element_type=F32)
    lane = lax.broadcasted_iota(jnp.int32, (CH, NZ), 1)
    for y in range(NY):
        part = product[:, y * NZ : (y + 1) * NZ]
        low = pltpu.roll(part[0:CH], 1, 1)
        high = pltpu.roll(part[2 * CH : 3 * CH], NZ - 1, 1)
        yield (
            part[CH : 2 * CH]
            + jnp.where(lane == 0, 0.0, low)
            + jnp.where(lane == NZ - 1, 0.0, high)
        )


def wait_for(ref, sem):
    pltpu.make_async_copy(ref, ref, sem).wait()


def kernel(
    real, xl, zs, co, planes, factor,
    grades, cot, weight, bias,
    act_out, gin_out, sum_out,
    gv, cv, wv, bv, work, turned_out, partial, field, dgrad, dshift, wslot, wf, wb, bias_col, slots,
    send1, recv1, recv2, piece,
    in_sem, w_send, w_recv, fs, fr, ds, dr, s1, r1, s2, r2, own_sem, seen1, seen2, seen3,
):
    strike = xl * zs * co
    quarter = xl * co
    members = real * quarter
    per = CH // members
    me_r, me_s = lax.axis_index("real"), lax.axis_index("strike")
    my_x, my_z, my_c = me_s // (zs * co), lax.rem(me_s // co, zs), lax.rem(me_s, co)
    me_m = me_r * quarter + my_x * co + my_c

    def member(m):
        q = lax.rem(m, quarter)
        return m // quarter, (q // co) * (zs * co) + my_z * co + lax.rem(q, co)

    load_g = pltpu.make_async_copy(grades.at[0], gv, in_sem.at[0])
    load_c = pltpu.make_async_copy(cot.at[0], cv, in_sem.at[1])
    load_w = pltpu.make_async_copy(weight, wv, in_sem.at[2])
    load_b = pltpu.make_async_copy(bias, bv, in_sem.at[3])
    load_w.start()
    load_b.start()
    load_g.start()
    load_c.start()

    barrier = pltpu.get_barrier_semaphore()

    wide_y = real // 2
    my_xh, my_y = me_r // wide_y, lax.rem(me_r, wide_y)

    def holder(k):
        across = k // wide_y
        to_r = lax.rem(my_xh + across, 2) * wide_y + lax.rem(my_y + lax.rem(k, wide_y), wide_y)
        return to_r, lax.rem(my_x + across, xl) * (zs * co) + my_z * co + my_c

    def beside(k):
        q = lax.rem(my_x * co + my_c + k, quarter)
        return me_r, (q // co) * (zs * co) + my_z * co + lax.rem(q, co)

    def along(k):
        return me_r, my_x * (zs * co) + lax.rem(my_z + k, zs) * co + my_c

    def tell(sem, device):
        pl.semaphore_signal(sem, inc=1, device_id=device, device_id_type=MESH)

    for k in range(1, real):
        tell(barrier, holder(k))
    for k in range(1, quarter):
        tell(barrier, beside(k))
    for k in (1, zs - 1):
        tell(barrier, along(k))

    @pl.when(me_s < strike - 1)
    def _():
        tell(barrier, (me_r, me_s + 1))

    @pl.when(me_s > 0)
    def _():
        tell(barrier, (me_r, me_s - 1))

    zero = jnp.zeros((CH, NZ), BF16)
    for x in range(planes + 2):
        for buf in (field, dgrad):
            buf[x, 0] = zero
            buf[x, NY + 1] = zero

    def clear(buf, x):
        def row(y, carry):
            buf[x, y + 1] = zero
            return carry

        lax.fori_loop(0, NY, row, 0, unroll=8)

    @pl.when(me_s == 0)
    def _():
        clear(field, 0)
        clear(dgrad, 0)

    @pl.when(me_s == strike - 1)
    def _():
        clear(field, planes + 1)
        clear(dgrad, planes + 1)

    rows = CH // real
    load_w.wait()
    load_b.wait()
    taps = wv[...].astype(F32)
    here = lax.broadcasted_iota(jnp.int32, (rows, rows), 0)
    there = lax.broadcasted_iota(jnp.int32, (rows, rows), 1)
    diagonal = jnp.where(here == there, jnp.broadcast_to(bv[...].astype(F32), (rows, rows)), 0.0)
    last = jnp.concatenate(
        [taps[:, 768:864], diagonal, jnp.zeros((rows, 160 - rows), F32)], axis=1
    )
    wslot[...] = jnp.concatenate(
        [taps[:, 0:256], taps[:, 256:512], taps[:, 512:768], last], axis=0
    ).astype(BF16)
    slots[me_r] = wslot[...]
    load_g.wait()
    for x in range(planes):

        def put(y, value, x=x):
            field[x + 1, y + 1] = value.astype(BF16)

        transpose_in(lambda c, x=x: gv[c, x], work, put)

    ends = (me_s == 0).astype(jnp.int32) + (me_s == strike - 1).astype(jnp.int32)
    pl.semaphore_wait(barrier, real - 1 + quarter - 1 + 4 - ends)

    for k in (1, zs - 1):
        tell(seen1, along(k))

    def send_weight(k, carry):
        pltpu.make_async_remote_copy(
            src_ref=wslot,
            dst_ref=slots.at[me_r],
            send_sem=w_send,
            recv_sem=w_recv,
            device_id=holder(k),
            device_id_type=MESH,
        ).start()
        return carry

    lax.fori_loop(1, real, send_weight, 0)

    def halo(buf, send, recv, up):
        here, there = (planes, 0) if up else (1, planes + 1)
        i = 0 if up else 1
        return pltpu.make_async_remote_copy(
            src_ref=buf.at[here, pl.ds(1, NY)],
            dst_ref=buf.at[there, pl.ds(1, NY)],
            send_sem=send.at[i],
            recv_sem=recv.at[i],
            device_id=(me_r, me_s + 1 if up else me_s - 1),
            device_id_type=MESH,
        )

    def send_halo(buf, send, recv):
        @pl.when(me_s < strike - 1)
        def _():
            halo(buf, send, recv, True).start()

        @pl.when(me_s > 0)
        def _():
            halo(buf, send, recv, False).start()

    def sent_halo(buf, send):
        @pl.when(me_s < strike - 1)
        def _():
            wait_for(buf.at[planes, pl.ds(1, NY)], send.at[0])

        @pl.when(me_s > 0)
        def _():
            wait_for(buf.at[1, pl.ds(1, NY)], send.at[1])

    def got_below(buf, recv):
        @pl.when(me_s > 0)
        def _():
            wait_for(buf.at[0, pl.ds(1, NY)], recv.at[0])

    def got_above(buf, recv):
        @pl.when(me_s < strike - 1)
        def _():
            wait_for(buf.at[planes + 1, pl.ds(1, NY)], recv.at[1])

    send_halo(field, fs, fr)

    pl.semaphore_wait(seen1, 2)
    for k in (2, zs - 2):
        tell(seen2, along(k))

    wait_for(slots.at[pl.ds(0, real - 1)], w_recv)
    gathered = slots[...].reshape(128, 256)
    row = lax.broadcasted_iota(jnp.int32, (128, 128), 0)
    col = lax.broadcasted_iota(jnp.int32, (128, 128), 1)
    out_row, group = lax.rem(row, CH), row // CH
    order = (
        col == (out_row // rows) * (4 * rows) + group * rows + lax.rem(out_row, rows)
    ).astype(BF16)
    whole = jnp.dot(order, gathered, preferred_element_type=F32)
    for c in range(3):
        ahead = []
        for ab in range(9):
            t = 3 * ab + c
            ahead.append(whole[(t // 8) * CH : (t // 8 + 1) * CH, (t % 8) * CH : (t % 8 + 1) * CH])
        wf[pl.ds(c * CH, CH), :] = jnp.concatenate(ahead, axis=1).astype(BF16)
    bias_col[...] = jnp.broadcast_to(
        jnp.sum(whole[96:128, 96 : 96 + rows], axis=1, keepdims=True), (CH, NZ)
    )

    lane = lax.broadcasted_iota(jnp.int32, (CH, NZ), 1)
    sides = ((1, 2), (0, 1))
    edges = ((0,), (2,))
    for x in range(planes):
        for y, value in enumerate(stencil(field, wf, x, sides[x])):
            partial[x, y] = value + bias_col[...]

    pl.semaphore_wait(seen2, 2)
    for k in range(1, quarter):
        tell(seen3, beside(k))

    load_c.wait()
    bias_sum = jnp.zeros((CH, NZ), F32)
    for x in range(planes):

        def spread(c, carry, x=x):
            work[pl.ds(pl.multiple_of(c * NY, NY), NY), :] = cv[c, x].astype(F32)
            return carry

        lax.fori_loop(0, CH, spread, 0, unroll=8)
        (got_below if x == 0 else got_above)(field, fr)
        for y, value in enumerate(stencil(field, wf, x, edges[x])):
            pre = value + partial[x, y]
            sig = jax.nn.sigmoid(pre)
            rise = pre * sig
            turned_out[pl.ds(x * CH * NY + y, CH, NY), :] = rise
            upstream = work[pl.ds(y, CH, NY), :]
            dpre = (upstream * (sig + rise * (1.0 - sig))).astype(BF16)
            dgrad[x + 1, y + 1] = dpre
            wide = dpre.astype(F32)
            bias_sum = bias_sum + wide
            before = jnp.where(lane == NZ - 1, 0.0, pltpu.roll(wide, NZ - 1, 1))
            after = jnp.where(lane == 0, 0.0, pltpu.roll(wide, 1, 1))
            dshift[x, y, 0:CH] = before.astype(BF16)
            dshift[x, y, CH : 2 * CH] = dpre
            dshift[x, y, 2 * CH : 3 * CH] = after.astype(BF16)

    send_halo(dgrad, ds, dr)
    total = None
    for x in range(planes):
        left = jnp.concatenate(
            [
                jnp.concatenate([field[x + a, y + b] for y in range(NY)], axis=1)
                for a in range(3)
                for b in range(3)
            ],
            axis=0,
        )
        right = jnp.concatenate([dshift[x, y] for y in range(NY)], axis=1)
        part = lax.dot_general(left, right, (((1,), (1,)), ((), ())), preferred_element_type=F32)
        total = part if total is None else total + part
    total = jnp.concatenate([total, jnp.zeros((9 * CH, CH), F32)], axis=1)
    total = jnp.concatenate([total, jnp.zeros((3 * CH, 4 * CH), F32)], axis=0)
    total = jnp.concatenate(
        [total[k * 128 : (k + 1) * 128].T for k in range(3)], axis=1
    )
    tails = []
    for c in range(3):
        block = total[c * CH : (c + 1) * CH]
        send1[pl.ds(2 * c, CH, 8), :] = block[:, 0:128]
        send1[pl.ds(2 * c + 1, CH, 8), :] = block[:, 128:256]
        tails.append(block[:, 256:288])
    send1[pl.ds(6, CH, 8), :] = jnp.concatenate(tails + [jnp.zeros((CH, 32), F32)], axis=1)
    send1[pl.ds(7, CH, 8), :] = bias_sum

    tile = per * 8

    def chunk(m):
        return send1.at[pl.ds(pl.multiple_of(m * tile, 8), tile)]

    def scatter(k, carry):
        m = lax.rem(me_m + k, members)
        pltpu.make_async_remote_copy(
            src_ref=chunk(m),
            dst_ref=recv1.at[me_m],
            send_sem=s1,
            recv_sem=r1,
            device_id=member(m),
            device_id_type=MESH,
        ).start()
        return carry

    lax.fori_loop(1, members, scatter, 0)
    own = pltpu.make_async_copy(chunk(me_m), recv1.at[me_m], own_sem)
    own.start()

    def pack(out):
        for x in range(planes):

            def channel(c, carry, x=x):
                rows_of = pl.ds(pl.multiple_of(x * CH * NY + c * NY, NY), NY)
                out[0, c, x] = turned_out[rows_of, :].astype(BF16)
                return carry

            lax.fori_loop(0, CH, channel, 0, unroll=8)

    pack(act_out)
    turned = jnp.concatenate([whole[:, :128].T, whole[:, 128:].T], axis=0)
    for c in range(3):
        back = []
        for ab in range(9):
            t = 26 - (3 * ab + c)
            back.append(turned[(t % 8) * CH : (t % 8 + 1) * CH, (t // 8) * CH : (t // 8 + 1) * CH])
        wb[pl.ds(c * CH, CH), :] = jnp.concatenate(back, axis=1).astype(BF16)
    for x in range(planes):
        for y, value in enumerate(stencil(dgrad, wb, x, sides[x])):
            partial[x, y] = value

    own.wait()
    wait_for(recv1.at[pl.ds(0, members - 1)], r1)
    plane_sum = recv1[0]
    for m in range(1, members):
        plane_sum = plane_sum + recv1[m]
    piece[...] = plane_sum.astype(BF16)
    recv2[me_s] = plane_sum.astype(BF16)

    pl.semaphore_wait(seen3, quarter - 1)

    def spread_sum(k, carry):
        pltpu.make_async_remote_copy(
            src_ref=piece,
            dst_ref=recv2.at[me_s],
            send_sem=s2,
            recv_sem=r2,
            device_id=(me_r, lax.rem(me_s + k, strike)),
            device_id_type=MESH,
        ).start()
        return carry

    lax.fori_loop(1, strike, spread_sum, 0)

    for x in range(planes):
        (got_below if x == 0 else got_above)(dgrad, dr)
        for y, value in enumerate(stencil(dgrad, wb, x, edges[x])):
            turned_out[pl.ds(x * CH * NY + y, CH, NY), :] = value + partial[x, y]
    pack(gin_out)

    wait_for(recv2.at[pl.ds(0, strike - 1)], r2)
    for xi in range(xl):
        for ci in range(co):
            value = recv2[xi * zs * co + ci].astype(F32)
            for z in range(1, zs):
                value = value + recv2[(xi * zs + z) * co + ci].astype(F32)
            sum_out[pl.ds((xi * co + ci) * tile, tile), :] = value * factor

    wait_for(slots.at[pl.ds(0, real - 1)], w_send)
    sent_halo(field, fs)
    sent_halo(dgrad, ds)
    wait_for(recv1.at[pl.ds(0, members - 1)], s1)
    wait_for(recv2.at[pl.ds(0, strike - 1)], s2)


def place(rows, act, gin, total, act_out, gin_out, weight_out, bias_out, taps_v, sums_v, sems):
    results = ((act, act_out), (gin, gin_out), (taps_v, weight_out), (sums_v, bias_out))
    moves = [
        pltpu.make_async_copy(held, out, sems.at[i]) for i, (held, out) in enumerate(results)
    ]
    moves[0].start()
    moves[1].start()
    parts = [total[pl.ds(g, rows, 8), :] for g in range(8)]
    taps = []
    for ab in range(9):
        for c in range(3):
            if ab < 8:
                source, at = parts[2 * c + ab // 4], (ab % 4) * 32
            else:
                source, at = parts[6], c * 32
            taps.append(source[:, at : at + 32])
    taps_v[...] = jnp.concatenate(taps, axis=1)
    sums = jnp.broadcast_to(jnp.sum(parts[7], axis=1, keepdims=True), (rows, 128))
    here = lax.broadcasted_iota(jnp.int32, (rows, 128), 0)
    there = lax.broadcasted_iota(jnp.int32, (rows, 128), 1)
    line = jnp.sum(jnp.where(here == there, sums, 0.0), axis=0, keepdims=True)
    sums_v[...] = line[:, :rows]
    moves[2].start()
    moves[3].start()
    for move in moves:
        move.wait()


def local(grades, cotangent, weight, bias, *, real, xl, zs, co):
    planes = grades.shape[2]
    strike = xl * zs * co
    members = real * xl * co
    per = CH // members
    rows = weight.shape[0]
    cells = real * strike * planes * NY * NZ
    factor = 1.0 / cells**0.5
    hbm = pl.BlockSpec(memory_space=pltpu.HBM)
    vmem = pl.BlockSpec(memory_space=pltpu.VMEM)
    block = jax.ShapeDtypeStruct((1, CH, planes, NY, NZ), BF16)
    scratch = [
        ((CH, planes, NY, NZ), BF16),
        ((CH, planes, NY, NZ), BF16),
        ((rows, 27 * CH), BF16),
        ((1, rows), BF16),
        ((CH * NY, NZ), F32),
        ((planes * CH * NY, NZ), F32),
        ((planes, NY, CH, NZ), F32),
        ((planes + 2, NY + 2, CH, NZ), BF16),
        ((planes + 2, NY + 2, CH, NZ), BF16),
        ((planes, NY, 3 * CH, NZ), BF16),
        ((rows * 4, 256), BF16),
        ((3 * CH, 9 * CH), BF16),
        ((3 * CH, 9 * CH), BF16),
        ((CH, NZ), F32),
        ((real, rows * 4, 256), BF16),
        ((CH * 8, 128), F32),
        ((members, per * 8, 128), F32),
        ((strike, per * 8, 128), BF16),
        ((per * 8, 128), BF16),
    ]
    pair, single = pltpu.SemaphoreType.DMA((2,)), pltpu.SemaphoreType.DMA
    act, gin, total = pl.pallas_call(
        functools.partial(kernel, real, xl, zs, co, planes, factor),
        out_shape=(block, block, jax.ShapeDtypeStruct((rows * 8, 128), F32)),
        in_specs=[hbm, hbm, hbm, hbm],
        out_specs=(vmem, vmem, vmem),
        scratch_shapes=[pltpu.VMEM(*each) for each in scratch]
        + [pltpu.SemaphoreType.DMA((4,)), single, single, pair, pair, pair, pair] + [single] * 5
        + [pltpu.SemaphoreType.REGULAR] * 3,
        compiler_params=pltpu.CompilerParams(
            collective_id=0, has_side_effects=True, vmem_limit_bytes=32 * 1024 * 1024
        ),
    )(
        pltpu.with_memory_space_constraint(grades, pltpu.HBM),
        pltpu.with_memory_space_constraint(cotangent, pltpu.HBM),
        pltpu.with_memory_space_constraint(weight, pltpu.HBM),
        pltpu.with_memory_space_constraint(bias.reshape(1, rows), pltpu.HBM),
    )
    act, gin, grad_weight, grad_bias = pl.pallas_call(
        functools.partial(place, rows),
        out_shape=(
            block,
            block,
            jax.ShapeDtypeStruct((rows, 27 * CH), F32),
            jax.ShapeDtypeStruct((1, rows), F32),
        ),
        in_specs=[vmem, vmem, vmem],
        out_specs=(hbm, hbm, hbm, hbm),
        scratch_shapes=[
            pltpu.VMEM((rows, 27 * CH), F32),
            pltpu.VMEM((1, rows), F32),
            pltpu.SemaphoreType.DMA((4,)),
        ],
        compiler_params=pltpu.CompilerParams(vmem_limit_bytes=4 * 1024 * 1024),
    )(act, gin, total)
    return act, gin, grad_weight, grad_bias.reshape(rows)


def solution(mesh):
    real, strike = mesh.shape["real"], mesh.shape["strike"]
    co = 2
    xl = 2 if strike >= 8 else 1
    zs = strike // (xl * co)
    split = P("real", None, "strike", None, None)
    specs = (split, split, P("real", None), P("real"))
    body = functools.partial(local, real=real, xl=xl, zs=zs, co=co)
    return jax.shard_map(body, mesh=mesh, in_specs=specs, out_specs=specs, check_vma=False)
```

```python
import functools

import jax
import jax.numpy as jnp
from jax import lax
from jax.experimental import pallas as pl
from jax.experimental.pallas import tpu as pltpu
from jax.sharding import PartitionSpec as P

MESH = pl.DeviceIdType.MESH
F32 = jnp.float32
BF16 = jnp.bfloat16
CH = 32
NY = 32
NZ = 128


def transpose_in(plane, work, put):
    def spread(c, carry):
        work[pl.ds(pl.multiple_of(c * NY, NY), NY), :] = plane(c).astype(F32)
        return carry

    lax.fori_loop(0, CH, spread, 0, unroll=8)

    def gather(y, carry):
        put(y, work[pl.ds(y, CH, NY), :])
        return carry

    lax.fori_loop(0, NY, gather, 0, unroll=8)


def rows_of(buf, slabs):
    pieces = []
    for slab in slabs:
        for b in range(3):
            pieces.append(jnp.concatenate([buf[slab, y + b] for y in range(NY)], axis=1))
    return jnp.concatenate(pieces, axis=0)


def gathered_z(part):
    lane = lax.broadcasted_iota(jnp.int32, (CH, NZ), 1)
    low = pltpu.roll(part[0:CH], 1, 1)
    high = pltpu.roll(part[2 * CH : 3 * CH], NZ - 1, 1)
    return (
        part[CH : 2 * CH]
        + jnp.where(lane == 0, 0.0, low)
        + jnp.where(lane == NZ - 1, 0.0, high)
    )


def inner_sums(buf, weights, partial, shift):
    product = jnp.dot(weights[...], rows_of(buf, (1, 2)), preferred_element_type=F32)
    for x in range(2):
        for y in range(NY):
            part = product[x * 3 * CH : (x + 1) * 3 * CH, y * NZ : (y + 1) * NZ]
            value = gathered_z(part)
            partial[x, y] = value if shift is None else value + shift


def outer_sums(buf, weights, x):
    product = jnp.dot(weights[x], rows_of(buf, (x * 3,)), preferred_element_type=F32)
    for y in range(NY):
        yield gathered_z(product[:, y * NZ : (y + 1) * NZ])


def lay_out(block, inner, outer):
    for c in range(3):
        taps = [block(c, ab) for ab in range(9)]
        for x in range(2):
            rows = pl.ds((x * 3 + c) * CH, CH)
            inner[rows, :] = jnp.concatenate(taps[3 - 3 * x : 9 - 3 * x], axis=1).astype(BF16)
            outer[x, pl.ds(c * CH, CH), :] = jnp.concatenate(
                taps[6 * x : 6 * x + 3], axis=1
            ).astype(BF16)


def wait_for(ref, sem):
    pltpu.make_async_copy(ref, ref, sem).wait()


def kernel(
    real, xl, zs, co, planes, factor,
    grades, cot, weight, bias,
    act_out, gin_out, sum_out,
    gv, cv, wv, bv, work, upstream, turned_out, partial, field, dgrad, dshift, wslot,
    wf_in, wf_out, wb_in, wb_out, bias_col, slots,
    send1, recv1, recv2, piece,
    in_sem, w_send, w_recv, fs, fr, ds, dr, s1, r1, s2, r2, own_sem, seen1, seen2, seen3,
):
    strike = xl * zs * co
    quarter = xl * co
    members = real * quarter
    per = CH // members
    me_r, me_s = lax.axis_index("real"), lax.axis_index("strike")
    my_x, my_z, my_c = me_s // (zs * co), lax.rem(me_s // co, zs), lax.rem(me_s, co)
    me_m = me_r * quarter + my_x * co + my_c

    def member(m):
        q = lax.rem(m, quarter)
        return m // quarter, (q // co) * (zs * co) + my_z * co + lax.rem(q, co)

    load_g = pltpu.make_async_copy(grades.at[0], gv, in_sem.at[0])
    load_c = pltpu.make_async_copy(cot.at[0], cv, in_sem.at[1])
    load_w = pltpu.make_async_copy(weight, wv, in_sem.at[2])
    load_b = pltpu.make_async_copy(bias, bv, in_sem.at[3])
    load_w.start()
    load_b.start()
    load_g.start()
    load_c.start()

    barrier = pltpu.get_barrier_semaphore()

    wide_y = real // 2
    my_xh, my_y = me_r // wide_y, lax.rem(me_r, wide_y)

    def holder(k):
        across = k // wide_y
        to_r = lax.rem(my_xh + across, 2) * wide_y + lax.rem(my_y + lax.rem(k, wide_y), wide_y)
        return to_r, lax.rem(my_x + across, xl) * (zs * co) + my_z * co + my_c

    def beside(k):
        q = lax.rem(my_x * co + my_c + k, quarter)
        return me_r, (q // co) * (zs * co) + my_z * co + lax.rem(q, co)

    def along(k):
        return me_r, my_x * (zs * co) + lax.rem(my_z + k, zs) * co + my_c

    def tell(sem, device):
        pl.semaphore_signal(sem, inc=1, device_id=device, device_id_type=MESH)

    for k in range(1, real):
        tell(barrier, holder(k))
    for k in range(1, quarter):
        tell(barrier, beside(k))
    for k in (1, zs - 1):
        tell(barrier, along(k))

    @pl.when(me_s < strike - 1)
    def _():
        tell(barrier, (me_r, me_s + 1))

    @pl.when(me_s > 0)
    def _():
        tell(barrier, (me_r, me_s - 1))

    zero = jnp.zeros((CH, NZ), BF16)
    for x in range(planes + 2):
        for buf in (field, dgrad):
            buf[x, 0] = zero
            buf[x, NY + 1] = zero

    def clear(buf, x):
        def row(y, carry):
            buf[x, y + 1] = zero
            return carry

        lax.fori_loop(0, NY, row, 0, unroll=8)

    @pl.when(me_s == 0)
    def _():
        clear(field, 0)
        clear(dgrad, 0)

    @pl.when(me_s == strike - 1)
    def _():
        clear(field, planes + 1)
        clear(dgrad, planes + 1)

    rows = CH // real
    load_w.wait()
    load_b.wait()
    taps = wv[...].astype(F32)
    here = lax.broadcasted_iota(jnp.int32, (rows, rows), 0)
    there = lax.broadcasted_iota(jnp.int32, (rows, rows), 1)
    diagonal = jnp.where(here == there, jnp.broadcast_to(bv[...].astype(F32), (rows, rows)), 0.0)
    last = jnp.concatenate(
        [taps[:, 768:864], diagonal, jnp.zeros((rows, 160 - rows), F32)], axis=1
    )
    wslot[...] = jnp.concatenate(
        [taps[:, 0:256], taps[:, 256:512], taps[:, 512:768], last], axis=0
    ).astype(BF16)
    slots[me_r] = wslot[...]
    load_g.wait()
    for x in range(planes):

        def put(y, value, x=x):
            field[x + 1, y + 1] = value.astype(BF16)

        transpose_in(lambda c, x=x: gv[c, x], work, put)

    ends = (me_s == 0).astype(jnp.int32) + (me_s == strike - 1).astype(jnp.int32)
    pl.semaphore_wait(barrier, real - 1 + quarter - 1 + 4 - ends)

    for k in (1, zs - 1):
        tell(seen1, along(k))

    def send_weight(k, carry):
        pltpu.make_async_remote_copy(
            src_ref=wslot,
            dst_ref=slots.at[me_r],
            send_sem=w_send,
            recv_sem=w_recv,
            device_id=holder(k),
            device_id_type=MESH,
        ).start()
        return carry

    lax.fori_loop(1, real, send_weight, 0)

    def halo(buf, send, recv, up):
        here, there = (planes, 0) if up else (1, planes + 1)
        i = 0 if up else 1
        return pltpu.make_async_remote_copy(
            src_ref=buf.at[here, pl.ds(1, NY)],
            dst_ref=buf.at[there, pl.ds(1, NY)],
            send_sem=send.at[i],
            recv_sem=recv.at[i],
            device_id=(me_r, me_s + 1 if up else me_s - 1),
            device_id_type=MESH,
        )

    def send_halo(buf, send, recv):
        @pl.when(me_s < strike - 1)
        def _():
            halo(buf, send, recv, True).start()

        @pl.when(me_s > 0)
        def _():
            halo(buf, send, recv, False).start()

    def sent_halo(buf, send):
        @pl.when(me_s < strike - 1)
        def _():
            wait_for(buf.at[planes, pl.ds(1, NY)], send.at[0])

        @pl.when(me_s > 0)
        def _():
            wait_for(buf.at[1, pl.ds(1, NY)], send.at[1])

    send_halo(field, fs, fr)

    load_c.wait()
    for x in range(planes):

        def put_cot(y, value, x=x):
            upstream[x, y] = value.astype(BF16)

        transpose_in(lambda c, x=x: cv[c, x], work, put_cot)

    pl.semaphore_wait(seen1, 2)
    for k in (2, zs - 2):
        tell(seen2, along(k))

    wait_for(slots.at[pl.ds(0, real - 1)], w_recv)
    gathered = slots[...].reshape(128, 256)
    row = lax.broadcasted_iota(jnp.int32, (128, 128), 0)
    col = lax.broadcasted_iota(jnp.int32, (128, 128), 1)
    out_row, group = lax.rem(row, CH), row // CH
    order = (
        col == (out_row // rows) * (4 * rows) + group * rows + lax.rem(out_row, rows)
    ).astype(BF16)
    whole = jnp.dot(order, gathered, preferred_element_type=F32)
    def forward_tap(c, ab):
        t = 3 * ab + c
        return whole[(t // 8) * CH : (t // 8 + 1) * CH, (t % 8) * CH : (t % 8 + 1) * CH]

    lay_out(forward_tap, wf_in, wf_out)
    bias_col[...] = jnp.broadcast_to(
        jnp.sum(whole[96:128, 96 : 96 + rows], axis=1, keepdims=True), (CH, NZ)
    )

    lane = lax.broadcasted_iota(jnp.int32, (CH, NZ), 1)
    inner_sums(field, wf_in, partial, bias_col[...])

    pl.semaphore_wait(seen2, 2)
    for k in range(1, quarter):
        tell(seen3, beside(k))

    def side(step):
        return lax.rem(step + 1 + my_c, 2)

    def got(buf, recv, x):
        @pl.when((x == 0) & (me_s > 0))
        def _():
            wait_for(buf.at[0, pl.ds(1, NY)], recv.at[0])

        @pl.when((x == 1) & (me_s < strike - 1))
        def _():
            wait_for(buf.at[planes + 1, pl.ds(1, NY)], recv.at[1])

    def forward(step, bias_sum):
        x = side(step)
        got(field, fr, x)
        for y, value in enumerate(outer_sums(field, wf_out, x)):
            pre = value + partial[x, y]
            sig = jax.nn.sigmoid(pre)
            rise = pre * sig
            turned_out[pl.ds(x * (CH * NY) + y, CH, NY), :] = rise
            slope = sig + rise * (1.0 - sig)
            dpre = (upstream[x, y].astype(F32) * slope).astype(BF16)
            dgrad[x + 1, y + 1] = dpre
            wide = dpre.astype(F32)
            bias_sum = bias_sum + wide
            before = jnp.where(lane == NZ - 1, 0.0, pltpu.roll(wide, NZ - 1, 1))
            after = jnp.where(lane == 0, 0.0, pltpu.roll(wide, 1, 1))
            dshift[x, y, 0:CH] = before.astype(BF16)
            dshift[x, y, CH : 2 * CH] = dpre
            dshift[x, y, 2 * CH : 3 * CH] = after.astype(BF16)
        return bias_sum

    bias_sum = lax.fori_loop(0, planes, forward, jnp.zeros((CH, NZ), F32))

    send_halo(dgrad, ds, dr)
    left = rows_of(field, (0, 1, 2, 3))
    right = jnp.concatenate(
        [jnp.concatenate([dshift[x, y] for y in range(NY)], axis=1) for x in range(2)], axis=0
    )
    both = lax.dot_general(left, right, (((1,), (1,)), ((), ())), preferred_element_type=F32)
    total = both[: 9 * CH, : 3 * CH] + both[3 * CH :, 3 * CH :]
    total = jnp.concatenate([total, jnp.zeros((9 * CH, CH), F32)], axis=1)
    total = jnp.concatenate([total, jnp.zeros((3 * CH, 4 * CH), F32)], axis=0)
    total = jnp.concatenate(
        [total[k * 128 : (k + 1) * 128].T for k in range(3)], axis=1
    )
    tails = []
    for c in range(3):
        block = total[c * CH : (c + 1) * CH]
        send1[pl.ds(2 * c, CH, 8), :] = block[:, 0:128]
        send1[pl.ds(2 * c + 1, CH, 8), :] = block[:, 128:256]
        tails.append(block[:, 256:288])
    send1[pl.ds(6, CH, 8), :] = jnp.concatenate(tails + [jnp.zeros((CH, 32), F32)], axis=1)
    send1[pl.ds(7, CH, 8), :] = bias_sum

    tile = per * 8

    def chunk(m):
        return send1.at[pl.ds(pl.multiple_of(m * tile, 8), tile)]

    def scatter(k, carry):
        m = lax.rem(me_m + k, members)
        pltpu.make_async_remote_copy(
            src_ref=chunk(m),
            dst_ref=recv1.at[me_m],
            send_sem=s1,
            recv_sem=r1,
            device_id=member(m),
            device_id_type=MESH,
        ).start()
        return carry

    lax.fori_loop(1, members, scatter, 0)
    own = pltpu.make_async_copy(chunk(me_m), recv1.at[me_m], own_sem)
    own.start()

    def pack(out):
        for x in range(planes):

            def channel(c, carry, x=x):
                rows_of = pl.ds(pl.multiple_of(x * CH * NY + c * NY, NY), NY)
                out[0, c, x] = turned_out[rows_of, :].astype(BF16)
                return carry

            lax.fori_loop(0, CH, channel, 0, unroll=8)

    pack(act_out)
    turned = jnp.concatenate([whole[:, :128].T, whole[:, 128:].T], axis=0)

    def backward_tap(c, ab):
        t = 26 - (3 * ab + c)
        return turned[(t % 8) * CH : (t % 8 + 1) * CH, (t // 8) * CH : (t // 8 + 1) * CH]

    lay_out(backward_tap, wb_in, wb_out)
    inner_sums(dgrad, wb_in, partial, None)

    own.wait()
    wait_for(recv1.at[pl.ds(0, members - 1)], r1)
    plane_sum = recv1[0]
    for m in range(1, members):
        plane_sum = plane_sum + recv1[m]
    piece[...] = plane_sum.astype(BF16)
    recv2[me_s] = plane_sum.astype(BF16)

    pl.semaphore_wait(seen3, quarter - 1)

    def spread_sum(k, carry):
        pltpu.make_async_remote_copy(
            src_ref=piece,
            dst_ref=recv2.at[me_s],
            send_sem=s2,
            recv_sem=r2,
            device_id=(me_r, lax.rem(me_s + k, strike)),
            device_id_type=MESH,
        ).start()
        return carry

    lax.fori_loop(1, strike, spread_sum, 0)

    def backward(step, carry):
        x = side(step)
        got(dgrad, dr, x)
        for y, value in enumerate(outer_sums(dgrad, wb_out, x)):
            turned_out[pl.ds(x * (CH * NY) + y, CH, NY), :] = value + partial[x, y]
        return carry

    lax.fori_loop(0, planes, backward, 0)
    pack(gin_out)

    wait_for(recv2.at[pl.ds(0, strike - 1)], r2)
    for xi in range(xl):
        for ci in range(co):
            value = recv2[xi * zs * co + ci].astype(F32)
            for z in range(1, zs):
                value = value + recv2[(xi * zs + z) * co + ci].astype(F32)
            sum_out[pl.ds((xi * co + ci) * tile, tile), :] = value * factor

    wait_for(slots.at[pl.ds(0, real - 1)], w_send)
    sent_halo(field, fs)
    sent_halo(dgrad, ds)
    wait_for(recv1.at[pl.ds(0, members - 1)], s1)
    wait_for(recv2.at[pl.ds(0, strike - 1)], s2)


def place(rows, act, gin, total, act_out, gin_out, weight_out, bias_out, taps_v, sums_v, sems):
    results = ((act, act_out), (gin, gin_out), (taps_v, weight_out), (sums_v, bias_out))
    moves = [
        pltpu.make_async_copy(held, out, sems.at[i]) for i, (held, out) in enumerate(results)
    ]
    moves[0].start()
    moves[1].start()
    parts = [total[pl.ds(g, rows, 8), :] for g in range(8)]
    taps = []
    for ab in range(9):
        for c in range(3):
            if ab < 8:
                source, at = parts[2 * c + ab // 4], (ab % 4) * 32
            else:
                source, at = parts[6], c * 32
            taps.append(source[:, at : at + 32])
    taps_v[...] = jnp.concatenate(taps, axis=1)
    sums = jnp.broadcast_to(jnp.sum(parts[7], axis=1, keepdims=True), (rows, 128))
    here = lax.broadcasted_iota(jnp.int32, (rows, 128), 0)
    there = lax.broadcasted_iota(jnp.int32, (rows, 128), 1)
    line = jnp.sum(jnp.where(here == there, sums, 0.0), axis=0, keepdims=True)
    sums_v[...] = line[:, :rows]
    moves[2].start()
    moves[3].start()
    for move in moves:
        move.wait()


def local(grades, cotangent, weight, bias, *, real, xl, zs, co):
    planes = grades.shape[2]
    strike = xl * zs * co
    members = real * xl * co
    per = CH // members
    rows = weight.shape[0]
    cells = real * strike * planes * NY * NZ
    factor = 1.0 / cells**0.5
    hbm = pl.BlockSpec(memory_space=pltpu.HBM)
    vmem = pl.BlockSpec(memory_space=pltpu.VMEM)
    block = jax.ShapeDtypeStruct((1, CH, planes, NY, NZ), BF16)
    scratch = [
        ((CH, planes, NY, NZ), BF16),
        ((CH, planes, NY, NZ), BF16),
        ((rows, 27 * CH), BF16),
        ((1, rows), BF16),
        ((CH * NY, NZ), F32),
        ((planes, NY, CH, NZ), BF16),
        ((planes * CH * NY, NZ), F32),
        ((planes, NY, CH, NZ), F32),
        ((planes + 2, NY + 2, CH, NZ), BF16),
        ((planes + 2, NY + 2, CH, NZ), BF16),
        ((planes, NY, 3 * CH, NZ), BF16),
        ((rows * 4, 256), BF16),
        ((6 * CH, 6 * CH), BF16),
        ((2, 3 * CH, 3 * CH), BF16),
        ((6 * CH, 6 * CH), BF16),
        ((2, 3 * CH, 3 * CH), BF16),
        ((CH, NZ), F32),
        ((real, rows * 4, 256), BF16),
        ((CH * 8, 128), F32),
        ((members, per * 8, 128), F32),
        ((strike, per * 8, 128), BF16),
        ((per * 8, 128), BF16),
    ]
    pair, single = pltpu.SemaphoreType.DMA((2,)), pltpu.SemaphoreType.DMA
    act, gin, total = pl.pallas_call(
        functools.partial(kernel, real, xl, zs, co, planes, factor),
        out_shape=(block, block, jax.ShapeDtypeStruct((rows * 8, 128), F32)),
        in_specs=[hbm, hbm, hbm, hbm],
        out_specs=(vmem, vmem, vmem),
        scratch_shapes=[pltpu.VMEM(*each) for each in scratch]
        + [pltpu.SemaphoreType.DMA((4,)), single, single, pair, pair, pair, pair] + [single] * 5
        + [pltpu.SemaphoreType.REGULAR] * 3,
        compiler_params=pltpu.CompilerParams(
            collective_id=0, has_side_effects=True, vmem_limit_bytes=32 * 1024 * 1024
        ),
    )(
        pltpu.with_memory_space_constraint(grades, pltpu.HBM),
        pltpu.with_memory_space_constraint(cotangent, pltpu.HBM),
        pltpu.with_memory_space_constraint(weight, pltpu.HBM),
        pltpu.with_memory_space_constraint(bias.reshape(1, rows), pltpu.HBM),
    )
    act, gin, grad_weight, grad_bias = pl.pallas_call(
        functools.partial(place, rows),
        out_shape=(
            block,
            block,
            jax.ShapeDtypeStruct((rows, 27 * CH), F32),
            jax.ShapeDtypeStruct((1, rows), F32),
        ),
        in_specs=[vmem, vmem, vmem],
        out_specs=(hbm, hbm, hbm, hbm),
        scratch_shapes=[
            pltpu.VMEM((rows, 27 * CH), F32),
            pltpu.VMEM((1, rows), F32),
            pltpu.SemaphoreType.DMA((4,)),
        ],
        compiler_params=pltpu.CompilerParams(vmem_limit_bytes=4 * 1024 * 1024),
    )(act, gin, total)
    return act, gin, grad_weight, grad_bias.reshape(rows)


def solution(mesh):
    real, strike = mesh.shape["real"], mesh.shape["strike"]
    co = 2
    xl = 2 if strike >= 8 else 1
    zs = strike // (xl * co)
    split = P("real", None, "strike", None, None)
    specs = (split, split, P("real", None), P("real"))
    body = functools.partial(local, real=real, xl=xl, zs=zs, co=co)
    return jax.shard_map(body, mesh=mesh, in_specs=specs, out_specs=specs, check_vma=False)
```
